512 devices in a mesh: fsdp: 32 (over z, core), tp: 16 (over x, y).
Axes of the slice: x: 4, y: 4, z: 16, core: 2. Of those that a mesh axis runs over, the one named last changes fastest.
Arguments:
- gradient: bfloat16 [8192, 28672], P('fsdp', 'tp'), may hold values from -6 to 6
- momentum: bfloat16 [8192, 28672], P('fsdp', 'tp'), may hold values from -6 to 6
- right_factor: bfloat16 [28672, 256], P(('tp', 'fsdp')), may hold values from -0.03125 to 0.03125
Outputs:
- update: bfloat16 [8192, 28672], P('fsdp', 'tp')
- new_momentum: bfloat16 [8192, 28672], P('fsdp', 'tp')
- new_right: bfloat16 [28672, 256], P(('tp', 'fsdp'))
The draws below stay inside these ranges and needn't reach their ends.
All inputs are finite; a program needn't handle non-finite values.
Results may differ from the reference program's by a relative error of at most 0.0085.
Values may be sent and summed in bfloat16 or wider, within the bound.
A program may use at most 64 MiB of HBM per device.

```python
import math
import jax
import jax.numpy as jnp
from jax import lax

D = 8192
FF = 28672
RANK = 256


level_variance = 0.34375


def shared_part(key, terms):
    sign_key, level_key = jax.random.split(key)
    signs = jax.random.randint(sign_key, (D, terms), 0, 2).astype(jnp.float32) * 2.0 - 1.0
    levels = jax.random.randint(level_key, (FF, terms), -32, 33).astype(jnp.float32) / 32.0
    product = jnp.dot(signs, levels.T, precision=lax.Precision.HIGHEST)
    return product * (1.0 / math.sqrt(terms * level_variance))


def column_ramp(ratio):
    place = jnp.arange(FF, dtype=jnp.float32) / float(FF)
    return jnp.exp((place - 0.5) * math.log(ratio)).reshape(1, FF)


def draw_gradient(key, part):
    shared = shared_part(key, max(RANK // 8, 1))
    key = jax.random.fold_in(key, 11)
    noise_key = jax.random.fold_in(key, 0)
    noise = jax.random.normal(noise_key, (D, FF), jnp.float32)
    mixed = (0.9 * shared + 0.5 * noise) * column_ramp(3.0)
    return jnp.clip(mixed, -6.0, 6.0).astype(jnp.bfloat16)


def draw_momentum(key, part):
    shared = shared_part(key, max(RANK // 8, 1))
    key = jax.random.fold_in(key, 12)
    noise_key = jax.random.fold_in(key, 0)
    noise = jax.random.normal(noise_key, (D, FF), jnp.float32)
    mixed = (0.8 * shared + 0.6 * noise) * column_ramp(3.0)
    return jnp.clip(mixed, -6.0, 6.0).astype(jnp.bfloat16)


def steps_of(own_key, shape, cuts, smallest, high):
    def one(dim, parts):
        steps = jax.random.uniform(jax.random.fold_in(jax.random.fold_in(own_key, 6), dim), (parts,), jnp.float32, smallest / len(cuts), high / len(cuts))
        return jnp.repeat(jnp.exp(steps), shape[dim] // parts).reshape((-1,) + (1,) * (len(shape) - dim - 1))

    factor_of = one(*cuts[0])
    for cut in cuts[1:]:
        factor_of = factor_of * one(*cut)
    return factor_of


def gaussian(own_key, shape, scale, most, pieces=(), held_as=jnp.bfloat16):
    array = scale * jax.random.normal(own_key, shape, jnp.float32)
    if pieces:
        array = array * steps_of(own_key, shape, pieces, -0.22, 0.18)
    return jnp.clip(array, -most, most).astype(held_as)


def setup_inputs(seed: int = 0) -> dict:
    keys = jax.random.split(jax.random.key(seed), 4)
    return {
        "gradient": draw_gradient(jax.random.fold_in(keys[3], 71), 0),
        "momentum": draw_momentum(jax.random.fold_in(keys[3], 71), 0),
        "right_factor": gaussian(keys[2], (FF, RANK), FF ** -0.5, 0.03125, ((0, 512),)),
    }


epsilon = 1e-06
feedback = 0.1

def reference(gradient, momentum, right_factor):
    blend = momentum.astype(jnp.float32) + gradient.astype(jnp.float32)
    blend_b = blend.astype(jnp.bfloat16)
    basis = jnp.dot(blend_b.astype(jnp.float32), right_factor.astype(jnp.float32), preferred_element_type=jnp.float32)
    gram_matrix = jnp.dot(basis.T, basis, precision=lax.Precision.HIGHEST)
    lower = jnp.linalg.cholesky(gram_matrix)
    ortho = jax.scipy.linalg.solve_triangular(lower, basis.T, lower=True).T
    ortho_b = ortho.astype(jnp.bfloat16)
    projected = jnp.dot(blend_b.T.astype(jnp.float32), ortho_b.astype(jnp.float32), preferred_element_type=jnp.float32)
    col_sums = lax.optimization_barrier(jnp.sum(projected * projected, axis=0))
    new_right = (projected * lax.rsqrt(col_sums + epsilon)).astype(jnp.bfloat16)
    projected_b = projected.astype(jnp.bfloat16)
    rank_term = jnp.dot(ortho_b.astype(jnp.float32), projected_b.T.astype(jnp.float32), preferred_element_type=jnp.float32)
    new_momentum = (blend - feedback * rank_term).astype(jnp.bfloat16)
    rms_scale = math.sqrt(D * FF / RANK)
    update = (rms_scale * jnp.dot(ortho_b.astype(jnp.float32), new_right.T.astype(jnp.float32), preferred_element_type=jnp.float32)).astype(jnp.bfloat16)
    return (update, new_momentum, new_right)
```

```python
import functools
import math

import jax
import jax.numpy as jnp
from jax import lax
from jax.experimental import pallas as pl
from jax.experimental.pallas import tpu as pltpu
from jax.sharding import PartitionSpec as P

D = 8192
FF = 28672
RANK = 256

epsilon = 1e-06
feedback = 0.1

F32 = jnp.float32
BF16 = jnp.bfloat16
MESH = pl.DeviceIdType.MESH
HIGHEST = lax.Precision.HIGHEST
LANES = 128
PIVOTS = 32
NEAR = (1, -1, 2, -2)
FAR = (5, -5)
RELAY_AT = 64
VMEM_LIMIT = 62 * 1024 * 1024


class Place:
    def __init__(self, chips, tensors):
        self.chips, self.tensors = chips, tensors
        self.f = lax.axis_index("fsdp")
        self.t = lax.axis_index("tp")
        self.z = lax.div(self.f, 2)
        self.c = lax.rem(self.f, 2)

    def chip(self, steps):
        return lax.rem(self.z + steps + self.chips, self.chips)

    def on_chip(self, z):
        return (z * 2 + self.c, self.t)

    def partner(self):
        return (self.z * 2 + 1 - self.c, self.t)

    def tensor(self, steps):
        return lax.rem(self.t + steps, self.tensors)


def remote(src, dst, send_sem, recv_sem, device):
    return pltpu.make_async_remote_copy(
        src_ref=src,
        dst_ref=dst,
        send_sem=send_sem,
        recv_sem=recv_sem,
        device_id=device,
        device_id_type=MESH,
    )


class Exchange:
    def __init__(self, place, chips, src, dst, arrived, send_sem, recv_sem, unroll):
        self.all = remote(arrived, arrived, send_sem, recv_sem, place.partner())

        def start(i, _):
            if chips:
                peer = place.chip(i)
                device = place.on_chip(peer)
            else:
                peer = place.tensor(i)
                device = (place.f, peer)
            remote(src(peer), dst, send_sem, recv_sem, device).start()
            return 0

        count = place.chips if chips else place.tensors
        if unroll:
            for i in range(1, count):
                start(i, 0)
        else:
            lax.fori_loop(1, count, start, 0)

    def wait_recv(self):
        self.all.wait_recv()

    def wait_send(self):
        self.all.wait_send()


class Gather:
    def __init__(self, place, slots, sems, recv_sem):
        self.place, self.slots = place, slots
        self.send_sem, self.send_part, self.recv_part = (sems.at[i] for i in range(3))
        self.recv_sem = recv_sem
        self.relayed = []

    def slot(self, chip):
        return self.slots.at[chip, self.place.c]

    def send(self, kind, chip, steps):
        ref = self.slot(chip)
        device = self.place.on_chip(self.place.chip(steps))
        remote(ref, ref, self.send_sem, self.recv_sem.at[kind], device).start()

    def arrived(self, kind, chip):
        ref = self.slot(chip)
        remote(ref, ref, self.send_sem, self.recv_sem.at[kind], self.place.partner()).wait_recv()

    def forward(self, chip):
        ref = self.slot(chip)
        remote(ref, ref, self.send_part, self.recv_part, self.place.partner()).start()

    def begin(self):
        for kind, steps in enumerate(FAR + NEAR):
            self.send(kind, self.place.z, steps)
        self.forward(self.place.z)

    def relay(self):
        place = self.place
        for i, far in enumerate(FAR):
            chip = place.chip(-far)
            self.arrived(i, chip)
            for j, near in enumerate(NEAR):
                self.send(6 + 4 * i + j, chip, near)
            self.forward(chip)
        self.send(14, place.chip(5 - 10 * place.c), 6 * place.c - 3)

    def finish(self):
        place = self.place
        for i, near in enumerate(NEAR):
            chip = place.chip(-near)
            self.arrived(2 + i, chip)
            self.forward(chip)
        for i, far in enumerate(FAR):
            for j, near in enumerate(NEAR):
                chip = place.chip(-far - near)
                self.arrived(6 + 4 * i + j, chip)
                self.forward(chip)
        self.arrived(14, place.chip(8))
        self.forward(place.chip(8))
        self.half().wait_recv()

    def half(self):
        ref = self.slots.at[:, 0]
        return remote(ref, ref, self.send_part, self.recv_part, self.place.partner())

    def drain(self):
        self.half().wait_send()
        ref = self.slots.at[: self.place.chips - 1, 0]
        remote(ref, ref, self.send_sem, self.recv_part, self.place.partner()).wait_send()


class Sum:
    def __init__(self, place, prepare, terms, relays, direct, sums, send_sem, recv_sem):
        self.place, self.terms = place, terms
        self.prepare = prepare
        self.relays, self.direct, self.sums = relays, direct, sums
        self.send_sem, self.recv_sem = send_sem, recv_sem
        self.started = {}

    def send(self, kind, src, into, steps):
        device = self.place.on_chip(self.place.chip(steps))
        copy = remote(src, into, self.send_sem, self.recv_sem.at[kind], device)
        copy.start()
        self.started[kind] = copy

    def begin(self):
        place = self.place
        for i, far in enumerate(FAR):
            for j, near in enumerate(NEAR):
                self.prepare(place.chip(near + far))
                self.send(4 * i + j, self.terms.at[place.chip(near + far)], self.relays.at[4 * i + j], near)
        self.prepare(place.chip(8))
        self.send(14, self.terms.at[place.chip(8)], self.relays.at[8], 3 - 6 * place.c)
        for j, near in enumerate(NEAR):
            self.prepare(place.chip(near))
            self.send(8 + j, self.terms.at[place.chip(near)], self.direct.at[j], near)
        for far in FAR:
            self.prepare(place.chip(far))
        self.prepare(place.z)

    def relay(self):
        for i, far in enumerate(FAR):
            value = self.terms[self.place.chip(far)]
            for j in range(4):
                self.started[4 * i + j].wait_recv()
                value = value + self.relays[4 * i + j]
            if i == 0:
                self.started[14].wait_recv()
            self.sums[i] = value + jnp.where(self.place.c == i, self.relays[8], 0.0)
            self.send(12 + i, self.sums.at[i], self.direct.at[4 + i], far)

    def finish(self):
        value = self.terms[self.place.z]
        for kind in range(8, 14):
            self.started[kind].wait_recv()
            value = value + self.direct[kind - 8]
        return value

    def drain(self):
        ref = self.terms.at[: self.place.chips - 1]
        remote(ref, ref, self.send_sem, self.recv_sem.at[0], self.place.partner()).wait_send()


def total(ref, count):
    value = ref[0]
    for i in range(1, count):
        value = value + ref[i]
    return value


def packed(value):
    return jnp.concatenate([value[:, :LANES], value[:, LANES:]], axis=0).astype(BF16)


def unpack(slots, chips, block, out, ready=None):
    quarter = chips // 4
    for k in range(chips):
        pair = [slots[k, core].astype(F32) for core in range(2)]
        for half in range(2):
            rows = jnp.concatenate([value[half * block : (half + 1) * block] for value in pair], axis=0)
            out[2 * block * k : 2 * block * (k + 1), half * LANES : (half + 1) * LANES] = rows.astype(BF16)
        if ready and (k + 1) % quarter == 0:
            ready(slice(2 * block * (k + 1 - quarter), 2 * block * (k + 1)))


def eliminate(left, right, scale, first):
    n = left.shape[0]
    tiles = n // LANES
    groups = PIVOTS // 8
    in_group = lax.broadcasted_iota(jnp.int32, (8, LANES), 0)
    tile0 = first // LANES
    left_tiles = list(range(tile0, tiles))
    right_tiles = list(range(0, tile0 + 1))

    def load(ref, g, tile):
        return ref[first + 8 * g : first + 8 * g + 8, tile * LANES : (tile + 1) * LANES]

    s = {tile: [load(left, g, tile) for g in range(groups)] for tile in left_tiles}
    m = {tile: [load(right, g, tile) for g in range(groups)] for tile in right_tiles}
    inverse = [jnp.zeros((8, LANES), F32) for _ in range(groups)]
    for sub in range(groups):
        lane = first + 8 * sub - tile0 * LANES
        column = [
            {
                g: jnp.broadcast_to(s[tile0][g][:, lane + j : lane + j + 1], (8, LANES))
                for g in range(sub, groups)
            }
            for j in range(8)
        ]
        for j in range(0, 8, 2):
            col0, col1 = column[j], column[j + 1]
            a = col0[sub][j : j + 1, :]
            b = col1[sub][j : j + 1, :]
            c = col1[sub][j + 1 : j + 2, :]
            recip0 = 1.0 / a
            recip1 = a * (1.0 / (a * c - b * b))
            lower = b * recip0
            inverse[sub] = jnp.where(in_group == j, recip0, jnp.where(in_group == j + 1, recip1, inverse[sub]))
            factors = {}
            for g in range(sub, groups):
                factor0 = col0[g] * recip0
                factor1 = (col1[g] - col0[g] * lower) * recip1
                if g == sub:
                    factor0 = jnp.where(in_group > j, factor0, 0.0)
                    factor1 = jnp.where(in_group > j + 1, factor1, 0.0)
                factors[g] = (factor0, factor1)

            def reduce(parts):
                row0 = parts[sub][j : j + 1, :]
                row1 = parts[sub][j + 1 : j + 2, :] - lower * row0
                for g, (factor0, factor1) in factors.items():
                    parts[g] = (parts[g] - factor0 * row0) - factor1 * row1

            for k in range(j + 2, 8):
                reduce(column[k])
            for tile in left_tiles:
                reduce(s[tile])
            for tile in right_tiles:
                reduce(m[tile])
    for g in range(groups):
        rows = slice(first + 8 * g, first + 8 * g + 8)
        scale[rows, :] = inverse[g]
        for tile in right_tiles:
            right[rows, tile * LANES : (tile + 1) * LANES] = m[tile][g]
    done = first + PIVOTS
    if done == n:
        return

    def joined(parts):
        return jnp.concatenate(parts, axis=0)

    lower0 = tile0 * LANES
    s_rows = {tile: joined(s[tile]) for tile in left_tiles}
    m_rows = {tile: joined(m[tile]) for tile in right_tiles}
    scaled = jnp.concatenate([s_rows[tile] * joined(inverse) for tile in left_tiles], axis=1)
    both = jnp.concatenate([s_rows[tile] for tile in left_tiles] + [m_rows[tile] for tile in right_tiles], axis=1)
    change = lax.dot_general(
        scaled, both, (((0,), (0,)), ((), ())), precision=HIGHEST, preferred_element_type=F32
    )
    below = slice(done - lower0, n - lower0)
    wide = len(left_tiles) * LANES
    left[done:, lower0:] = left[done:, lower0:] - change[below, :wide]
    right[done:, : len(right_tiles) * LANES] = right[done:, : len(right_tiles) * LANES] - change[below, wide:]


def main_kernel(
    chips, tensors,
    g_ref, m_ref, r_ref, ortho_out, projected_out, own_out, norm_out,
    g_here, m_here, r_here, blend_b, slots, right_all, partial, parts, basis, gram, other, pieces, gathered,
    left, right, scale, product, from_partner, terms, relays, direct, relay_sums, projected_slots,
    squares, other_squares, square_parts, square_rows, ortho, projected, own_rows, norm,
    load_sem, sems_r, recv_r, send_q, recv_q, send_h, recv_h, sems_p, recv_p, send_t, recv_t, send_z, recv_z, send_o, recv_o, store_sem,
):
    place = Place(chips, tensors)
    rows, width = g_ref.shape
    block, rank = r_ref.shape
    share = rows // tensors
    piece = rank // tensors // 2
    tile = math.gcd(width, 256)
    drains = []
    barrier = pltpu.get_barrier_semaphore()

    def greet(device):
        pl.semaphore_signal(barrier, inc=1, device_id=device, device_id_type=MESH)

    def greet_chip(i, _):
        greet(place.on_chip(place.chip(i)))
        return 0

    def greet_tensor(i, _):
        greet((place.f, place.tensor(i)))
        return 0

    loads = [
        pltpu.make_async_copy(src, dst, load_sem.at[i])
        for i, (src, dst) in enumerate(((r_ref, r_here), (g_ref, g_here), (m_ref, m_here)))
    ]
    loads[0].start()
    greet(place.partner())
    lax.fori_loop(1, chips, greet_chip, 0)
    lax.fori_loop(1, tensors, greet_tensor, 0)
    for load in loads[1:]:
        load.start()
    loads[0].wait()
    slots[place.z, place.c] = packed(r_here[...].astype(F32))
    pl.semaphore_wait(barrier, tensors + chips - 1)

    stores = []

    def store(src, dst):
        copy = pltpu.make_async_copy(src, dst, store_sem.at[len(stores)])
        copy.start()
        stores.append(copy)

    def exchange(chips, index, src, dst, arrived, unroll=True):
        sems = (send_z, recv_z) if chips else (send_t, recv_t)
        new = Exchange(place, chips, src, dst, arrived, sems[0].at[index], sems[1].at[index], unroll)
        drains.append(new.wait_send)
        return new

    def swap(index, src, dst):
        new = remote(src, dst, send_o.at[index], recv_o.at[index], place.partner())
        new.start()
        drains.append(new.wait_send)
        return new

    with jax.named_scope("gather_right"):
        gather = Gather(place, slots, sems_r, recv_r)
        gather.begin()
        drains.append(gather.drain)
        for load in loads[1:]:
            load.wait()
        for j in range(0, width, tile):
            columns = slice(j, j + tile)
            blend_b[:, columns] = (m_here[:, columns].astype(F32) + g_here[:, columns].astype(F32)).astype(BF16)
        gather.relay()
        gather.finish()
    unpack(slots, chips, block, right_all)
    partial[...] = jnp.dot(blend_b[...], right_all[...], preferred_element_type=F32)

    def share_of(ref, t):
        return ref.at[pl.ds(pl.multiple_of(t * share, share), share), :]

    with jax.named_scope("sum_basis"):
        work = exchange(False, 0, lambda t: share_of(partial, t), parts.at[place.t], parts.at[: tensors - 1])
        parts[place.t] = share_of(partial, place.t)[...]
        work.wait_recv()
        mine = share_of(basis, place.t)
        mine[...] = total(parts, tensors)
        exchange(False, 1, lambda t: mine, mine, basis.at[: rows - share]).wait_recv()

    contract_rows = (((0,), (0,)), ((), ()))
    contract_columns = (((1,), (1,)), ((), ()))
    value = basis[...]
    gram[...] = lax.dot_general(value, value, contract_rows, precision=HIGHEST, preferred_element_type=F32)

    def piece_of(core):
        return gram.at[pl.ds(pl.multiple_of((place.t * 2 + core) * piece, piece), piece), :]

    gram_swap = swap(0, piece_of(1 - place.c), other)

    splits = []
    for _ in range(3):
        splits.append(value.astype(BF16))
        value = value - splits[-1].astype(F32)
    basis_b = jnp.concatenate(splits, axis=1)
    for j in range(0, width, tile):
        part = lax.dot_general(blend_b[:, j : j + tile], basis_b, contract_rows, preferred_element_type=F32)
        part = part[:, :rank] + part[:, rank : 2 * rank] + part[:, 2 * rank :]
        at = j
        while at < j + tile:
            chunk, skip = divmod(at, block)
            most = min(block - skip, j + tile - at)
            product[chunk // 2, chunk % 2, skip : skip + most, :] = part[at - j : at - j + most]
            at += most
    order = [place.chip(near + far) for far in FAR for near in NEAR] + [place.chip(8)]
    order += [place.chip(steps) for steps in NEAR + FAR] + [place.z]
    halves = []
    for i, chip in enumerate(order):
        half = remote(
            product.at[chip, 1 - place.c], from_partner.at[chip], send_h.at[0], recv_h.at[i], place.partner()
        )
        half.start()
        halves.append(half)

    gram_swap.wait_recv()
    pieces[place.z] = piece_of(place.c)[...] + other[...]
    with jax.named_scope("sum_gram"):
        gram_work = exchange(
            True, 0, lambda z: pieces.at[place.z], pieces.at[place.z], pieces.at[: chips - 1]
        )
        waiting = list(halves)

        def add_cores(chip):
            waiting.pop(0).wait_recv()
            terms[chip] = product[chip, place.c] + from_partner[chip]

        chip_sum = Sum(place, add_cores, terms, relays, direct, relay_sums, send_q.at[0], recv_q)
        chip_sum.begin()
        for drain in drains:
            drain()
        drains.clear()
        drains.append(chip_sum.drain)
        drains.append(
            remote(from_partner, from_partner, send_h.at[0], recv_h.at[0], place.partner()).wait_send
        )
        gram_work.wait_recv()
        gathered[place.c, place.t] = total(pieces, chips)
        own = gathered.at[place.c, place.t]
        exchange(False, 2, lambda t: own, own, gathered.at[0, : tensors - 1]).wait_recv()
        swap(1, gathered.at[place.c], gathered.at[place.c]).wait_recv()
    for t in range(tensors):
        for core in range(2):
            at = (t * 2 + core) * piece
            left[at : at + piece, :] = gathered[core, t]

    at_row = lax.broadcasted_iota(jnp.int32, (rank, rank), 0)
    at_column = lax.broadcasted_iota(jnp.int32, (rank, rank), 1)
    right[...] = jnp.where(at_row == at_column, 1.0, 0.0).astype(F32)
    value = left[...]
    diagonal = jnp.where(at_row == at_column, value, 0.0)
    to_unit = lax.rsqrt(jnp.sum(diagonal, axis=0, keepdims=True))
    left[...] = value * lax.rsqrt(jnp.sum(diagonal, axis=1, keepdims=True)) * to_unit
    with jax.named_scope("factor"):
        for first in range(0, rank, PIVOTS):
            if first == RELAY_AT:
                chip_sum.relay()
            eliminate(left, right, scale, first)
    inverse_lower = jnp.concatenate(
        [right[:, at : at + LANES] * jnp.sqrt(scale[...]) for at in range(0, rank, LANES)], axis=1
    ) * to_unit
    value = lax.dot_general(
        chip_sum.finish(), inverse_lower, contract_columns, precision=HIGHEST, preferred_element_type=F32
    )
    projected_slots[place.z, place.c] = packed(value)
    with jax.named_scope("gather_projected"):
        gather = Gather(place, projected_slots, sems_p, recv_p)
        gather.begin()
        drains.append(gather.drain)
        squares[...] = jnp.sum((value * value).reshape(block // 8, 8, rank), axis=0)
        square_swap = swap(3, squares, other_squares)
        own_rows[...] = value
        store(own_rows, own_out)
        ortho[...] = lax.dot_general(
            basis[...], inverse_lower, contract_columns, precision=HIGHEST, preferred_element_type=F32
        ).astype(BF16)
        store(ortho, ortho_out)
        square_swap.wait_recv()
        square_parts[place.t] = squares[...] + other_squares[...]
        mine = square_parts.at[place.t]
        work = exchange(False, 3, lambda t: mine, mine, square_parts.at[: tensors - 1], False)
        gather.relay()
        work.wait_recv()
        square_rows[place.z] = jnp.sum(total(square_parts, tensors), axis=0, keepdims=True)
        mine_row = square_rows.at[place.z]
        work = exchange(True, 1, lambda z: mine_row, mine_row, square_rows.at[: chips - 1], False)
        gather.finish()
        work.wait_recv()
    norm[...] = jnp.broadcast_to(lax.rsqrt(total(square_rows, chips) + epsilon), norm.shape)
    store(norm, norm_out)
    unpack(
        projected_slots, chips, block, projected,
        lambda rows: store(projected.at[rows, :], projected_out.at[rows, :]),
    )
    for drain in drains:
        drain()
    for copy in stores:
        copy.wait()


def output_kernel(
    g_ref, m_ref, o_ref, p_ref, own_ref, norm_ref, update_out, momentum_out, right_out,
    g_here, m_here, p_here, update, momentum, o_here, own_here, norm_here, right_here,
    load_sem, store_sem, small_sem,
):
    width = g_ref.shape[1]
    step = math.gcd(width, 256)
    spans = [slice(at, min(at + 2 * step, width)) for at in range(0, width, 2 * step)]
    small = [
        pltpu.make_async_copy(src, dst, small_sem.at[i])
        for i, (src, dst) in enumerate(((o_ref, o_here), (norm_ref, norm_here), (own_ref, own_here)))
    ]
    for copy in small:
        copy.start()
    loads = []
    for i, span in enumerate(spans):
        copies = [
            pltpu.make_async_copy(p_ref.at[span, :], p_here.at[span, :], load_sem.at[0, i]),
            pltpu.make_async_copy(g_ref.at[:, span], g_here.at[:, span], load_sem.at[1, i]),
            pltpu.make_async_copy(m_ref.at[:, span], m_here.at[:, span], load_sem.at[2, i]),
        ]
        for copy in copies:
            copy.start()
        loads.append(copies)
    contract = (((1,), (1,)), ((), ()))
    for copy in small:
        copy.wait()
    ortho_b = o_here[...]
    norm = norm_here[0:1, :]
    right_here[...] = (own_here[...] * norm).astype(BF16)
    stores = [pltpu.make_async_copy(right_here, right_out, small_sem.at[3])]
    stores[0].start()
    for i, span in enumerate(spans):
        for copy in loads[i]:
            copy.wait()
        for at in range(span.start, span.stop, step):
            columns = slice(at, at + step)
            projected = p_here[columns, :]
            term = lax.dot_general(ortho_b, projected, contract, preferred_element_type=F32)
            blend = m_here[:, columns].astype(F32) + g_here[:, columns].astype(F32)
            momentum[:, columns] = (blend - feedback * term).astype(BF16)
            new_right = (projected.astype(F32) * norm).astype(BF16)
            term = lax.dot_general(ortho_b, new_right, contract, preferred_element_type=F32)
            update[:, columns] = (math.sqrt(D * FF / RANK) * term).astype(BF16)
        copies = [
            pltpu.make_async_copy(momentum.at[:, span], momentum_out.at[:, span], store_sem.at[0, i]),
            pltpu.make_async_copy(update.at[:, span], update_out.at[:, span], store_sem.at[1, i]),
        ]
        for copy in copies:
            copy.start()
        stores += copies
    for copy in stores:
        copy.wait()


def shards(chips, tensors, gradient, momentum, right_factor):
    rows, width = gradient.shape
    block, rank = right_factor.shape
    piece = rank // tensors // 2
    anywhere = pl.BlockSpec(memory_space=pl.ANY)

    def dma(*shape):
        return pltpu.SemaphoreType.DMA(shape)

    ortho_b, projected, own, norm = pl.pallas_call(
        functools.partial(main_kernel, chips, tensors),
        out_shape=[
            jax.ShapeDtypeStruct((rows, rank), BF16),
            jax.ShapeDtypeStruct((width, rank), BF16),
            jax.ShapeDtypeStruct((block, rank), F32),
            jax.ShapeDtypeStruct((8, rank), F32),
        ],
        in_specs=[anywhere] * 3,
        out_specs=[anywhere] * 4,
        scratch_shapes=[
            pltpu.VMEM((rows, width), BF16),
            pltpu.VMEM((rows, width), BF16),
            pltpu.VMEM((block, rank), BF16),
            pltpu.VMEM((rows, width), BF16),
            pltpu.VMEM((chips, 2, 2 * block, LANES), BF16),
            pltpu.VMEM((width, rank), BF16),
            pltpu.VMEM((rows, rank), F32),
            pltpu.VMEM((tensors, rows // tensors, rank), F32),
            pltpu.VMEM((rows, rank), F32),
            pltpu.VMEM((rank, rank), F32),
            pltpu.VMEM((piece, rank), F32),
            pltpu.VMEM((chips, piece, rank), F32),
            pltpu.VMEM((2, tensors, piece, rank), F32),
            pltpu.VMEM((rank, rank), F32),
            pltpu.VMEM((rank, rank), F32),
            pltpu.VMEM((rank, LANES), F32),
            pltpu.VMEM((chips, 2, block, rank), F32),
            pltpu.VMEM((chips, block, rank), F32),
            pltpu.VMEM((chips, block, rank), F32),
            pltpu.VMEM((9, block, rank), F32),
            pltpu.VMEM((6, block, rank), F32),
            pltpu.VMEM((2, block, rank), F32),
            pltpu.VMEM((chips, 2, 2 * block, LANES), BF16),
            pltpu.VMEM((8, rank), F32),
            pltpu.VMEM((8, rank), F32),
            pltpu.VMEM((tensors, 8, rank), F32),
            pltpu.VMEM((chips, 1, rank), F32),
            pltpu.VMEM((rows, rank), BF16),
            pltpu.VMEM((width, rank), BF16),
            pltpu.VMEM((block, rank), F32),
            pltpu.VMEM((8, rank), F32),
            dma(3), dma(3), dma(chips - 1), dma(1), dma(chips - 1), dma(1), dma(chips), dma(3), dma(chips - 1),
            dma(4), dma(4), dma(2), dma(2), dma(4), dma(4), dma(7),
        ],
        compiler_params=pltpu.CompilerParams(
            collective_id=0, has_side_effects=True, vmem_limit_bytes=VMEM_LIMIT
        ),
        name="main",
    )(gradient, momentum, right_factor)

    spans = -(-width // (2 * math.gcd(width, 256)))
    whole = pltpu.VMEM((rows, width), BF16)
    return pl.pallas_call(
        output_kernel,
        out_shape=[
            jax.ShapeDtypeStruct((rows, width), BF16),
            jax.ShapeDtypeStruct((rows, width), BF16),
            jax.ShapeDtypeStruct((block, rank), BF16),
        ],
        in_specs=[anywhere] * 6,
        out_specs=[anywhere] * 3,
        scratch_shapes=[
            whole, whole, pltpu.VMEM((width, rank), BF16), whole, whole,
            pltpu.VMEM((rows, rank), BF16), pltpu.VMEM((block, rank), F32), pltpu.VMEM((8, rank), F32),
            pltpu.VMEM((block, rank), BF16),
            dma(3, spans), dma(2, spans), dma(4),
        ],
        compiler_params=pltpu.CompilerParams(vmem_limit_bytes=VMEM_LIMIT),
        name="output",
    )(gradient, momentum, ortho_b, projected, own, norm)


def solution(mesh):
    chips, tensors = mesh.shape["fsdp"] // 2, mesh.shape["tp"]
    in_specs = (P("fsdp", "tp"), P("fsdp", "tp"), P(("tp", "fsdp"), None))
    out_specs = (P("fsdp", "tp"), P("fsdp", "tp"), P(("tp", "fsdp"), None))
    return jax.shard_map(
        functools.partial(shards, chips, tensors),
        mesh=mesh, in_specs=in_specs, out_specs=out_specs, check_vma=False,
    )
```

```python
import functools
import math

import jax
import jax.numpy as jnp
from jax import lax
from jax.experimental import pallas as pl
from jax.experimental.pallas import tpu as pltpu
from jax.sharding import PartitionSpec as P

D = 8192
FF = 28672
RANK = 256

epsilon = 1e-06
feedback = 0.1

F32 = jnp.float32
BF16 = jnp.bfloat16
MESH = pl.DeviceIdType.MESH
HIGHEST = lax.Precision.HIGHEST
LANES = 128
PIVOTS = 64
NEAR = (1, -1, 2, -2)
FAR = (5, -5)
RELAY_AT = 64
VMEM_LIMIT = 62 * 1024 * 1024


class Place:
    def __init__(self, chips, tensors):
        self.chips, self.tensors = chips, tensors
        self.f = lax.axis_index("fsdp")
        self.t = lax.axis_index("tp")
        self.z = lax.div(self.f, 2)
        self.c = lax.rem(self.f, 2)

    def chip(self, steps):
        return lax.rem(self.z + steps + self.chips, self.chips)

    def on_chip(self, z):
        return (z * 2 + self.c, self.t)

    def partner(self):
        return (self.z * 2 + 1 - self.c, self.t)

    def tensor(self, steps):
        return lax.rem(self.t + steps, self.tensors)


def remote(src, dst, send_sem, recv_sem, device):
    return pltpu.make_async_remote_copy(
        src_ref=src,
        dst_ref=dst,
        send_sem=send_sem,
        recv_sem=recv_sem,
        device_id=device,
        device_id_type=MESH,
    )


class Exchange:
    def __init__(self, place, chips, src, dst, arrived, send_sem, recv_sem, unroll):
        self.all = remote(arrived, arrived, send_sem, recv_sem, place.partner())

        def start(i, _):
            if chips:
                peer = place.chip(i)
                device = place.on_chip(peer)
            else:
                peer = place.tensor(i)
                device = (place.f, peer)
            remote(src(peer), dst, send_sem, recv_sem, device).start()
            return 0

        count = place.chips if chips else place.tensors
        if unroll:
            for i in range(1, count):
                start(i, 0)
        else:
            lax.fori_loop(1, count, start, 0)

    def wait_recv(self):
        self.all.wait_recv()

    def wait_send(self):
        self.all.wait_send()


class Gather:
    def __init__(self, place, slots, sems, recv_sem):
        self.place, self.slots = place, slots
        self.send_sem, self.send_part, self.recv_part = (sems.at[i] for i in range(3))
        self.recv_sem = recv_sem
        self.relayed = []

    def slot(self, chip):
        return self.slots.at[chip, self.place.c]

    def send(self, kind, chip, steps):
        ref = self.slot(chip)
        device = self.place.on_chip(self.place.chip(steps))
        remote(ref, ref, self.send_sem, self.recv_sem.at[kind], device).start()

    def arrived(self, kind, chip):
        ref = self.slot(chip)
        remote(ref, ref, self.send_sem, self.recv_sem.at[kind], self.place.partner()).wait_recv()

    def forward(self, chip):
        ref = self.slot(chip)
        remote(ref, ref, self.send_part, self.recv_part, self.place.partner()).start()

    def begin(self):
        for kind, steps in enumerate(FAR + NEAR):
            self.send(kind, self.place.z, steps)
        self.forward(self.place.z)

    def relay(self):
        place = self.place
        for i, far in enumerate(FAR):
            chip = place.chip(-far)
            self.arrived(i, chip)
            for j, near in enumerate(NEAR):
                self.send(6 + 4 * i + j, chip, near)
            self.forward(chip)
        self.send(14, place.chip(5 - 10 * place.c), 6 * place.c - 3)

    def finish(self):
        place = self.place
        for i, near in enumerate(NEAR):
            chip = place.chip(-near)
            self.arrived(2 + i, chip)
            self.forward(chip)
        for i, far in enumerate(FAR):
            for j, near in enumerate(NEAR):
                chip = place.chip(-far - near)
                self.arrived(6 + 4 * i + j, chip)
                self.forward(chip)
        self.arrived(14, place.chip(8))
        self.forward(place.chip(8))
        self.half().wait_recv()

    def half(self):
        ref = self.slots.at[:, 0]
        return remote(ref, ref, self.send_part, self.recv_part, self.place.partner())

    def drain(self):
        self.half().wait_send()
        ref = self.slots.at[: self.place.chips - 1, 0]
        remote(ref, ref, self.send_sem, self.recv_part, self.place.partner()).wait_send()


class Sum:
    def __init__(self, place, terms, relays, direct, sums, send_sem, recv_sem):
        self.place, self.terms = place, terms
        self.relays, self.direct, self.sums = relays, direct, sums
        self.send_sem, self.recv_sem = send_sem, recv_sem
        self.started = {}

    def send(self, kind, src, into, steps):
        device = self.place.on_chip(self.place.chip(steps))
        copy = remote(src, into, self.send_sem, self.recv_sem.at[kind], device)
        copy.start()
        self.started[kind] = copy

    def begin(self):
        place = self.place
        for i, far in enumerate(FAR):
            for j, near in enumerate(NEAR):
                self.send(4 * i + j, self.terms.at[place.chip(near + far)], self.relays.at[4 * i + j], near)
        self.send(14, self.terms.at[place.chip(8)], self.relays.at[8], 3 - 6 * place.c)
        for j, near in enumerate(NEAR):
            self.send(8 + j, self.terms.at[place.chip(near)], self.direct.at[j], near)

    def relay(self):
        for i, far in enumerate(FAR):
            value = self.terms[self.place.chip(far)]
            for j in range(4):
                self.started[4 * i + j].wait_recv()
                value = value + self.relays[4 * i + j]
            if i == 0:
                self.started[14].wait_recv()
            self.sums[i] = value + jnp.where(self.place.c == i, self.relays[8], 0.0)
            self.send(12 + i, self.sums.at[i], self.direct.at[4 + i], far)

    def finish(self):
        value = self.terms[self.place.z]
        for kind in range(8, 14):
            self.started[kind].wait_recv()
            value = value + self.direct[kind - 8]
        return value

    def drain(self):
        ref = self.terms.at[: self.place.chips - 1]
        remote(ref, ref, self.send_sem, self.recv_sem.at[0], self.place.partner()).wait_send()


def total(ref, count):
    value = ref[0]
    for i in range(1, count):
        value = value + ref[i]
    return value


def packed(value):
    return jnp.concatenate([value[:, :LANES], value[:, LANES:]], axis=0).astype(BF16)


def unpack(slots, chips, block, out, ready=None):
    quarter = chips // 4
    for k in range(chips):
        pair = [slots[k, core].astype(F32) for core in range(2)]
        for half in range(2):
            rows = jnp.concatenate([value[half * block : (half + 1) * block] for value in pair], axis=0)
            out[2 * block * k : 2 * block * (k + 1), half * LANES : (half + 1) * LANES] = rows.astype(BF16)
        if ready and (k + 1) % quarter == 0:
            ready(slice(2 * block * (k + 1 - quarter), 2 * block * (k + 1)))


def eliminate(left, right, scale, first):
    n = left.shape[0]
    tiles = n // LANES
    groups = PIVOTS // 8
    in_group = lax.broadcasted_iota(jnp.int32, (8, LANES), 0)
    tile0 = first // LANES
    left_tiles = list(range(tile0, tiles))
    right_tiles = list(range(0, tile0 + 1))

    def load(ref, g, tile):
        return ref[first + 8 * g : first + 8 * g + 8, tile * LANES : (tile + 1) * LANES]

    s = {tile: [load(left, g, tile) for g in range(groups)] for tile in left_tiles}
    m = {tile: [load(right, g, tile) for g in range(groups)] for tile in right_tiles}
    inverse = [jnp.zeros((8, LANES), F32) for _ in range(groups)]
    for sub in range(groups):
        lane = first + 8 * sub - tile0 * LANES
        column = [
            {
                g: jnp.broadcast_to(s[tile0][g][:, lane + j : lane + j + 1], (8, LANES))
                for g in range(sub, groups)
            }
            for j in range(8)
        ]
        for j in range(0, 8, 2):
            col0, col1 = column[j], column[j + 1]
            a = col0[sub][j : j + 1, :]
            b = col1[sub][j : j + 1, :]
            c = col1[sub][j + 1 : j + 2, :]
            recip0 = 1.0 / a
            recip1 = a * (1.0 / (a * c - b * b))
            lower = b * recip0
            inverse[sub] = jnp.where(in_group == j, recip0, jnp.where(in_group == j + 1, recip1, inverse[sub]))
            factors = {}
            for g in range(sub, groups):
                factor0 = col0[g] * recip0
                factor1 = (col1[g] - col0[g] * lower) * recip1
                if g == sub:
                    factor0 = jnp.where(in_group > j, factor0, 0.0)
                    factor1 = jnp.where(in_group > j + 1, factor1, 0.0)
                factors[g] = (factor0, factor1)

            def reduce(parts):
                row0 = parts[sub][j : j + 1, :]
                row1 = parts[sub][j + 1 : j + 2, :] - lower * row0
                for g, (factor0, factor1) in factors.items():
                    parts[g] = (parts[g] - factor0 * row0) - factor1 * row1

            for k in range(j + 2, 8):
                reduce(column[k])
            for tile in left_tiles:
                reduce(s[tile])
            for tile in right_tiles:
                reduce(m[tile])
    for g in range(groups):
        rows = slice(first + 8 * g, first + 8 * g + 8)
        scale[rows, :] = inverse[g]
        for tile in right_tiles:
            right[rows, tile * LANES : (tile + 1) * LANES] = m[tile][g]
    done = first + PIVOTS
    if done == n:
        return

    def joined(parts):
        return jnp.concatenate(parts, axis=0)

    lower0 = tile0 * LANES
    s_rows = {tile: joined(s[tile]) for tile in left_tiles}
    m_rows = {tile: joined(m[tile]) for tile in right_tiles}
    scaled = jnp.concatenate([s_rows[tile] * joined(inverse) for tile in left_tiles], axis=1)
    both = jnp.concatenate([s_rows[tile] for tile in left_tiles] + [m_rows[tile] for tile in right_tiles], axis=1)
    change = lax.dot_general(
        scaled, both, (((0,), (0,)), ((), ())), precision=HIGHEST, preferred_element_type=F32
    )
    below = slice(done - lower0, n - lower0)
    wide = len(left_tiles) * LANES
    left[done:, lower0:] = left[done:, lower0:] - change[below, :wide]
    right[done:, : len(right_tiles) * LANES] = right[done:, : len(right_tiles) * LANES] - change[below, wide:]


def main_kernel(
    chips, tensors,
    g_ref, m_ref, r_ref, ortho_out, projected_out, own_out, norm_out,
    g_here, m_here, r_here, blend_b, slots, right_all, partial, parts, basis, gram, other, pieces, gathered,
    left, right, scale, product, from_partner, terms, relays, direct, relay_sums, projected_slots,
    squares, other_squares, square_parts, square_rows, ortho, projected, own_rows, norm,
    load_sem, sems_r, recv_r, send_q, recv_q, sems_p, recv_p, send_t, recv_t, send_z, recv_z, send_o, recv_o, store_sem,
):
    place = Place(chips, tensors)
    rows, width = g_ref.shape
    block, rank = r_ref.shape
    share = rows // tensors
    piece = rank // tensors // 2
    tile = math.gcd(width, 256)
    drains = []
    barrier = pltpu.get_barrier_semaphore()

    def greet(device):
        pl.semaphore_signal(barrier, inc=1, device_id=device, device_id_type=MESH)

    def greet_chip(i, _):
        greet(place.on_chip(place.chip(i)))
        return 0

    def greet_tensor(i, _):
        greet((place.f, place.tensor(i)))
        return 0

    loads = [
        pltpu.make_async_copy(src, dst, load_sem.at[i])
        for i, (src, dst) in enumerate(((r_ref, r_here), (g_ref, g_here), (m_ref, m_here)))
    ]
    loads[0].start()
    greet(place.partner())
    lax.fori_loop(1, chips, greet_chip, 0)
    lax.fori_loop(1, tensors, greet_tensor, 0)
    for load in loads[1:]:
        load.start()
    loads[0].wait()
    slots[place.z, place.c] = packed(r_here[...].astype(F32))
    pl.semaphore_wait(barrier, tensors + chips - 1)

    stores = []

    def store(src, dst):
        copy = pltpu.make_async_copy(src, dst, store_sem.at[len(stores)])
        copy.start()
        stores.append(copy)

    def exchange(chips, index, src, dst, arrived, unroll=True):
        sems = (send_z, recv_z) if chips else (send_t, recv_t)
        new = Exchange(place, chips, src, dst, arrived, sems[0].at[index], sems[1].at[index], unroll)
        drains.append(new.wait_send)
        return new

    def swap(index, src, dst):
        new = remote(src, dst, send_o.at[index], recv_o.at[index], place.partner())
        new.start()
        drains.append(new.wait_send)
        return new

    with jax.named_scope("gather_right"):
        gather = Gather(place, slots, sems_r, recv_r)
        gather.begin()
        drains.append(gather.drain)
        for load in loads[1:]:
            load.wait()
        for j in range(0, width, tile):
            columns = slice(j, j + tile)
            blend_b[:, columns] = (m_here[:, columns].astype(F32) + g_here[:, columns].astype(F32)).astype(BF16)
        gather.relay()
        gather.finish()
    unpack(slots, chips, block, right_all)
    partial[...] = jnp.dot(blend_b[...], right_all[...], preferred_element_type=F32)

    def share_of(ref, t):
        return ref.at[pl.ds(pl.multiple_of(t * share, share), share), :]

    with jax.named_scope("sum_basis"):
        work = exchange(False, 0, lambda t: share_of(partial, t), parts.at[place.t], parts.at[: tensors - 1])
        parts[place.t] = share_of(partial, place.t)[...]
        work.wait_recv()
        mine = share_of(basis, place.t)
        mine[...] = total(parts, tensors)
        exchange(False, 1, lambda t: mine, mine, basis.at[: rows - share]).wait_recv()

    contract_rows = (((0,), (0,)), ((), ()))
    contract_columns = (((1,), (1,)), ((), ()))
    value = basis[...]
    gram[...] = lax.dot_general(value, value, contract_rows, precision=HIGHEST, preferred_element_type=F32)

    def piece_of(core):
        return gram.at[pl.ds(pl.multiple_of((place.t * 2 + core) * piece, piece), piece), :]

    gram_swap = swap(0, piece_of(1 - place.c), other)

    gram_swap.wait_recv()
    pieces[place.z] = piece_of(place.c)[...] + other[...]
    with jax.named_scope("sum_gram"):
        gram_work = exchange(
            True, 0, lambda z: pieces.at[place.z], pieces.at[place.z], pieces.at[: chips - 1]
        )
        splits = []
        for _ in range(3):
            splits.append(value.astype(BF16))
            value = value - splits[-1].astype(F32)
        basis_b = jnp.concatenate(splits, axis=1)
        for j in range(0, width, tile):
            part = lax.dot_general(blend_b[:, j : j + tile], basis_b, contract_rows, preferred_element_type=F32)
            part = part[:, :rank] + part[:, rank : 2 * rank] + part[:, 2 * rank :]
            at = j
            while at < j + tile:
                chunk, skip = divmod(at, block)
                most = min(block - skip, j + tile - at)
                product[chunk // 2, chunk % 2, skip : skip + most, :] = part[at - j : at - j + most]
                at += most
        product_swap = swap(2, product.at[:, 1 - place.c], from_partner)
        for drain in drains:
            drain()
        drains.clear()
        product_swap.wait_recv()

        def add_cores(k, _):
            terms[k] = product[k, place.c] + from_partner[k]
            return 0

        lax.fori_loop(0, chips, add_cores, 0)
        chip_sum = Sum(place, terms, relays, direct, relay_sums, send_q.at[0], recv_q)
        chip_sum.begin()
        drains.append(chip_sum.drain)
        gram_work.wait_recv()
        gathered[place.c, place.t] = total(pieces, chips)
        own = gathered.at[place.c, place.t]
        exchange(False, 2, lambda t: own, own, gathered.at[0, : tensors - 1]).wait_recv()
        swap(1, gathered.at[place.c], gathered.at[place.c]).wait_recv()
    for t in range(tensors):
        for core in range(2):
            at = (t * 2 + core) * piece
            left[at : at + piece, :] = gathered[core, t]

    at_row = lax.broadcasted_iota(jnp.int32, (rank, rank), 0)
    at_column = lax.broadcasted_iota(jnp.int32, (rank, rank), 1)
    right[...] = jnp.where(at_row == at_column, 1.0, 0.0).astype(F32)
    value = left[...]
    diagonal = jnp.where(at_row == at_column, value, 0.0)
    to_unit = lax.rsqrt(jnp.sum(diagonal, axis=0, keepdims=True))
    left[...] = value * lax.rsqrt(jnp.sum(diagonal, axis=1, keepdims=True)) * to_unit
    with jax.named_scope("factor"):
        for first in range(0, rank, PIVOTS):
            if first == RELAY_AT:
                chip_sum.relay()
            eliminate(left, right, scale, first)
    inverse_lower = jnp.concatenate(
        [right[:, at : at + LANES] * jnp.sqrt(scale[...]) for at in range(0, rank, LANES)], axis=1
    ) * to_unit
    value = lax.dot_general(
        chip_sum.finish(), inverse_lower, contract_columns, precision=HIGHEST, preferred_element_type=F32
    )
    projected_slots[place.z, place.c] = packed(value)
    with jax.named_scope("gather_projected"):
        gather = Gather(place, projected_slots, sems_p, recv_p)
        gather.begin()
        drains.append(gather.drain)
        squares[...] = jnp.sum((value * value).reshape(block // 8, 8, rank), axis=0)
        square_swap = swap(3, squares, other_squares)
        own_rows[...] = value
        store(own_rows, own_out)
        ortho[...] = lax.dot_general(
            basis[...], inverse_lower, contract_columns, precision=HIGHEST, preferred_element_type=F32
        ).astype(BF16)
        store(ortho, ortho_out)
        square_swap.wait_recv()
        square_parts[place.t] = squares[...] + other_squares[...]
        mine = square_parts.at[place.t]
        work = exchange(False, 3, lambda t: mine, mine, square_parts.at[: tensors - 1], False)
        gather.relay()
        work.wait_recv()
        square_rows[place.z] = jnp.sum(total(square_parts, tensors), axis=0, keepdims=True)
        mine_row = square_rows.at[place.z]
        work = exchange(True, 1, lambda z: mine_row, mine_row, square_rows.at[: chips - 1], False)
        gather.finish()
        work.wait_recv()
    norm[...] = jnp.broadcast_to(lax.rsqrt(total(square_rows, chips) + epsilon), norm.shape)
    store(norm, norm_out)
    unpack(
        projected_slots, chips, block, projected,
        lambda rows: store(projected.at[rows, :], projected_out.at[rows, :]),
    )
    for drain in drains:
        drain()
    for copy in stores:
        copy.wait()


def output_kernel(
    g_ref, m_ref, o_ref, p_ref, own_ref, norm_ref, update_out, momentum_out, right_out,
    g_here, m_here, p_here, update, momentum, o_here, own_here, norm_here, right_here,
    load_sem, store_sem, small_sem,
):
    width = g_ref.shape[1]
    step = math.gcd(width, 256)
    spans = [slice(at, min(at + 2 * step, width)) for at in range(0, width, 2 * step)]
    small = [
        pltpu.make_async_copy(src, dst, small_sem.at[i])
        for i, (src, dst) in enumerate(((o_ref, o_here), (norm_ref, norm_here), (own_ref, own_here)))
    ]
    for copy in small:
        copy.start()
    loads = []
    for i, span in enumerate(spans):
        copies = [
            pltpu.make_async_copy(p_ref.at[span, :], p_here.at[span, :], load_sem.at[0, i]),
            pltpu.make_async_copy(g_ref.at[:, span], g_here.at[:, span], load_sem.at[1, i]),
            pltpu.make_async_copy(m_ref.at[:, span], m_here.at[:, span], load_sem.at[2, i]),
        ]
        for copy in copies:
            copy.start()
        loads.append(copies)
    contract = (((1,), (1,)), ((), ()))
    for copy in small:
        copy.wait()
    ortho_b = o_here[...]
    norm = norm_here[0:1, :]
    right_here[...] = (own_here[...] * norm).astype(BF16)
    stores = [pltpu.make_async_copy(right_here, right_out, small_sem.at[3])]
    stores[0].start()
    for i, span in enumerate(spans):
        for copy in loads[i]:
            copy.wait()
        for at in range(span.start, span.stop, step):
            columns = slice(at, at + step)
            projected = p_here[columns, :]
            term = lax.dot_general(ortho_b, projected, contract, preferred_element_type=F32)
            blend = m_here[:, columns].astype(F32) + g_here[:, columns].astype(F32)
            momentum[:, columns] = (blend - feedback * term).astype(BF16)
            new_right = (projected.astype(F32) * norm).astype(BF16)
            term = lax.dot_general(ortho_b, new_right, contract, preferred_element_type=F32)
            update[:, columns] = (math.sqrt(D * FF / RANK) * term).astype(BF16)
        copies = [
            pltpu.make_async_copy(momentum.at[:, span], momentum_out.at[:, span], store_sem.at[0, i]),
            pltpu.make_async_copy(update.at[:, span], update_out.at[:, span], store_sem.at[1, i]),
        ]
        for copy in copies:
            copy.start()
        stores += copies
    for copy in stores:
        copy.wait()


def shards(chips, tensors, gradient, momentum, right_factor):
    rows, width = gradient.shape
    block, rank = right_factor.shape
    piece = rank // tensors // 2
    anywhere = pl.BlockSpec(memory_space=pl.ANY)

    def dma(*shape):
        return pltpu.SemaphoreType.DMA(shape)

    ortho_b, projected, own, norm = pl.pallas_call(
        functools.partial(main_kernel, chips, tensors),
        out_shape=[
            jax.ShapeDtypeStruct((rows, rank), BF16),
            jax.ShapeDtypeStruct((width, rank), BF16),
            jax.ShapeDtypeStruct((block, rank), F32),
            jax.ShapeDtypeStruct((8, rank), F32),
        ],
        in_specs=[anywhere] * 3,
        out_specs=[anywhere] * 4,
        scratch_shapes=[
            pltpu.VMEM((rows, width), BF16),
            pltpu.VMEM((rows, width), BF16),
            pltpu.VMEM((block, rank), BF16),
            pltpu.VMEM((rows, width), BF16),
            pltpu.VMEM((chips, 2, 2 * block, LANES), BF16),
            pltpu.VMEM((width, rank), BF16),
            pltpu.VMEM((rows, rank), F32),
            pltpu.VMEM((tensors, rows // tensors, rank), F32),
            pltpu.VMEM((rows, rank), F32),
            pltpu.VMEM((rank, rank), F32),
            pltpu.VMEM((piece, rank), F32),
            pltpu.VMEM((chips, piece, rank), F32),
            pltpu.VMEM((2, tensors, piece, rank), F32),
            pltpu.VMEM((rank, rank), F32),
            pltpu.VMEM((rank, rank), F32),
            pltpu.VMEM((rank, LANES), F32),
            pltpu.VMEM((chips, 2, block, rank), F32),
            pltpu.VMEM((chips, block, rank), F32),
            pltpu.VMEM((chips, block, rank), F32),
            pltpu.VMEM((9, block, rank), F32),
            pltpu.VMEM((6, block, rank), F32),
            pltpu.VMEM((2, block, rank), F32),
            pltpu.VMEM((chips, 2, 2 * block, LANES), BF16),
            pltpu.VMEM((8, rank), F32),
            pltpu.VMEM((8, rank), F32),
            pltpu.VMEM((tensors, 8, rank), F32),
            pltpu.VMEM((chips, 1, rank), F32),
            pltpu.VMEM((rows, rank), BF16),
            pltpu.VMEM((width, rank), BF16),
            pltpu.VMEM((block, rank), F32),
            pltpu.VMEM((8, rank), F32),
            dma(3), dma(3), dma(chips - 1), dma(1), dma(chips - 1), dma(3), dma(chips - 1),
            dma(4), dma(4), dma(2), dma(2), dma(4), dma(4), dma(7),
        ],
        compiler_params=pltpu.CompilerParams(
            collective_id=0, has_side_effects=True, vmem_limit_bytes=VMEM_LIMIT
        ),
        name="main",
    )(gradient, momentum, right_factor)

    spans = -(-width // (2 * math.gcd(width, 256)))
    whole = pltpu.VMEM((rows, width), BF16)
    return pl.pallas_call(
        output_kernel,
        out_shape=[
            jax.ShapeDtypeStruct((rows, width), BF16),
            jax.ShapeDtypeStruct((rows, width), BF16),
            jax.ShapeDtypeStruct((block, rank), BF16),
        ],
        in_specs=[anywhere] * 6,
        out_specs=[anywhere] * 3,
        scratch_shapes=[
            whole, whole, pltpu.VMEM((width, rank), BF16), whole, whole,
            pltpu.VMEM((rows, rank), BF16), pltpu.VMEM((block, rank), F32), pltpu.VMEM((8, rank), F32),
            pltpu.VMEM((block, rank), BF16),
            dma(3, spans), dma(2, spans), dma(4),
        ],
        compiler_params=pltpu.CompilerParams(vmem_limit_bytes=VMEM_LIMIT),
        name="output",
    )(gradient, momentum, ortho_b, projected, own, norm)


def solution(mesh):
    chips, tensors = mesh.shape["fsdp"] // 2, mesh.shape["tp"]
    in_specs = (P("fsdp", "tp"), P("fsdp", "tp"), P(("tp", "fsdp"), None))
    out_specs = (P("fsdp", "tp"), P("fsdp", "tp"), P(("tp", "fsdp"), None))
    return jax.shard_map(
        functools.partial(shards, chips, tensors),
        mesh=mesh, in_specs=in_specs, out_specs=out_specs, check_vma=False,
    )
```
